32 devices in a mesh: dp: 4 (over y, x), expert: 8 (over z, core).
Axes of the slice: x: 2, y: 2, z: 4, core: 2. Of those that a mesh axis runs over, the one named last changes fastest.
Arguments:
- patches: bfloat16 [4096, 1024], P(('dp', 'expert')), may hold values from -6 to 6
- expert_ids: int32 [4096, 2], P(('dp', 'expert')), may hold values from 0 to 7, all different within a row; in each aligned block of 128 rows (0 to 127, 128 to 255, ...) at most 64 rows name the same one
- gate_weights: float32 [4096, 2], P(('dp', 'expert')), may hold values from 0.2 to 1
- conv_weight: float32 [49, 1024], replicated, may hold values from -2 to 2
- conv_bias: float32 [1024], replicated, may hold values from -6 to 6
- ln_gain: float32 [1024], replicated, may hold values from 0.1 to 1.9
- ln_shift: float32 [1024], replicated, may hold values from -6 to 6
- w_in: bfloat16 [8, 1024, 1024], P('expert', 'dp'), may hold values from -0.1875 to 0.1875
- w_out: bfloat16 [8, 1024, 1024], P('expert', 'dp'), may hold values from -0.1875 to 0.1875
- grad_mixed: bfloat16 [4096, 1024], P(('dp', 'expert')), may hold values from -6 to 6
Outputs:
- mixed: bfloat16 [4096, 1024], P(('dp', 'expert'))
- grad_input: float32 [4096, 1024], P(('dp', 'expert'))
- grad_w_in: float32 [8, 1024, 1024], P('expert', 'dp')
- grad_w_out: float32 [8, 1024, 1024], P('expert', 'dp')
The draws below stay inside these ranges and needn't reach their ends.
Inputs may be any that keep to these rules, and one draw needn't show every extreme that they name: `expert_ids`: the two ids of a row differ. Within the 128 rows of one device no expert is named more than 64 times, a bound that some block reaches in every draw.
All inputs are finite; a program needn't handle non-finite values.
Results may differ from the reference program's by a relative error of at most 0.013.
Values may be sent and summed in bfloat16 or wider, within the bound.
A program may use at most 64 MiB of HBM per device.

```python
import math
from functools import partial
import jax
import jax.numpy as jnp
import numpy as np
from jax import lax

D = 1024
EXP_HID = 1024
KSIZE = 7
TOP = 2
IMG_W = 16
IMG_H = 8
TOK_DEV = 128
EXPERTS = 8
CAP = 64
TOKENS = 4096
N_DP = 4
N_EXPERT = 8


def steps_of(stream_key, extent, shards, least, high):
    def one(axis_at, parts):
        heights = jax.random.uniform(jax.random.fold_in(jax.random.fold_in(stream_key, 6), axis_at), (parts,), jnp.float32, least / len(shards), high / len(shards))
        return jnp.repeat(jnp.exp(heights), extent[axis_at] // parts).reshape((-1,) + (1,) * (len(extent) - axis_at - 1))

    gain = one(*shards[0])
    for cut in shards[1:]:
        gain = gain * one(*cut)
    return gain


def deal_out(own_key, own, number, rows, number_of, top, reach, skew):
    order = jax.random.permutation(own_key, number_of)
    heavy_load, usual = portions_of(number_of, rows * top, reach, skew, True), portions_of(number_of, rows * top, reach, skew, False)
    places = jnp.arange(number_of)

    def named(sizes, turn):
        used = int((sizes > 0).sum())
        fixed = max(1, used // 4)
        moved = fixed + (places - fixed + turn * (used - fixed)) % max(1, number_of - fixed)
        return jnp.zeros((number_of,), jnp.int32).at[order[jnp.where(places < fixed, places, moved)]].set(jnp.asarray(sizes, jnp.int32))

    sizes = jnp.where(number % 4 == 0, named(heavy_load, number // 4), named(usual, number - number // 4 - 1))
    mixed = jax.random.permutation(jax.random.fold_in(own, 3), number_of)
    giver, receiver = mixed[0:number_of // 2 * 2:2], mixed[1:number_of // 2 * 2:2]
    slack = jnp.minimum(sizes[giver] - 1, reach - sizes[receiver]) // 2
    slack = jnp.where((giver == order[0]) | (receiver == order[0]) | (sizes[receiver] == 0), 0, jnp.maximum(slack, 0))
    moved = jax.random.randint(jax.random.fold_in(own, 4), (number_of // 2,), 0, 1 << 20) % (slack + 1)
    sizes = sizes.at[giver].add(-moved).at[receiver].add(moved)
    labels = jnp.searchsorted(jnp.cumsum(sizes), jnp.arange(rows * top), side="right").astype(jnp.int32)
    listing = labels.reshape(top, rows).T
    listing = listing[jax.random.permutation(jax.random.fold_in(own, 1), rows)]
    turn = jax.random.randint(jax.random.fold_in(own, 2), (rows, 1), 0, top)
    return jnp.take_along_axis(listing, (jnp.arange(top)[None, :] + turn) % top, axis=1)


def portions_of(count, total, bound, lean, full):
    portions = [(1 << 20) // math.isqrt(standing ** lean) + 1 for standing in range(1, count + 1)]
    largest = bound if full else min(bound, max(-(-total // count), total * portions[0] // sum(portions)))
    least = 1 if total - largest >= count - 1 else 0
    holding, surplus = [largest] + [least] * (count - 1), total - largest - least * (count - 1)
    while surplus > 0:
        movable = [i for i in range(1, count) if holding[i] < largest] or [i for i in range(1, count) if holding[i] < bound]
        pool, left = sum([portions[i] for i in movable]), surplus
        for i in movable:
            extra = min(bound - holding[i], max(1, left * portions[i] // pool), surplus)
            holding[i] = holding[i] + extra
            surplus = surplus - extra
    return np.array(holding)


def bell_draw(own_key, shape, deviation, most, shards=(), kind=jnp.bfloat16):
    drawn = deviation * jax.random.normal(own_key, shape, jnp.float32)
    if shards:
        drawn = drawn * steps_of(own_key, shape, shards, -0.22, 0.18)
    return jnp.clip(drawn, -most, most).astype(kind)


def setup_inputs(seed: int = 0) -> dict:
    keys = jax.random.split(jax.random.key(seed), 11)
    patches = bell_draw(keys[0], (TOKENS, D), 1.0, 6.0, ((0, 32),))
    expert_ids_keys = jax.random.split(jax.random.fold_in(keys[1], 1), TOKENS // TOK_DEV)
    expert_ids_turns = jax.random.permutation(jax.random.fold_in(keys[1], 3), TOKENS // TOK_DEV)
    expert_ids = jax.vmap(lambda own, number: deal_out(jax.random.fold_in(keys[1], 2), own, number, TOK_DEV, EXPERTS, TOP, CAP, 2))(expert_ids_keys, expert_ids_turns).reshape((TOKENS, TOP))
    gate_weights = jnp.clip(0.2 + 0.8 * jax.random.uniform(keys[2], (TOKENS, TOP), jnp.float32) ** steps_of(keys[2], (TOKENS, TOP), ((0, 32),), -0.2, 0.2), 0.2, 1.0)
    conv_weight = bell_draw(keys[3], (KSIZE * KSIZE, D), 0.15, 2.0, (), jnp.float32)
    conv_bias = bell_draw(keys[4], (D,), 0.5, 6.0, (), jnp.float32)
    ln_gain = jnp.clip(1.0 + 0.18 * jax.random.normal(keys[5], (D,), jnp.float32), 0.1, 1.9)
    ln_shift = bell_draw(keys[6], (D,), 0.5, 6.0, (), jnp.float32)
    w_in = bell_draw(keys[7], (EXPERTS, D, EXP_HID), D ** -0.5, 0.1875, ((0, 8), (1, 4)))
    w_out = bell_draw(keys[8], (EXPERTS, D, EXP_HID), EXP_HID ** -0.5, 0.1875, ((0, 8), (1, 4)))
    grad_mixed = bell_draw(keys[9], (TOKENS, D), 1.0, 6.0, ((0, 32),))
    return dict(patches=patches, expert_ids=expert_ids, gate_weights=gate_weights, conv_weight=conv_weight, conv_bias=conv_bias, ln_gain=ln_gain, ln_shift=ln_shift, w_in=w_in, w_out=w_out, grad_mixed=grad_mixed)


EPS = 1e-06

def front(images, conv_weight, conv_bias, ln_gain, ln_shift):
    half = KSIZE // 2
    padded = jnp.pad(images, ((0, 0), (half, half), (half, half), (0, 0)))
    total = jnp.zeros_like(images) + conv_bias
    for row in range(KSIZE):
        for col in range(KSIZE):
            total = total + padded[:, row:row + IMG_H, col:col + IMG_W, :] * conv_weight[row * KSIZE + col]
    mean = lax.optimization_barrier(jnp.mean(total, axis=-1, keepdims=True))
    centred = total - mean
    spread = lax.optimization_barrier(jnp.mean(centred * centred, axis=-1, keepdims=True))
    return centred * lax.rsqrt(spread + EPS) * ln_gain + ln_shift

def slot_positions(ids, capacity, count):
    flat = ids.reshape(-1)
    table = (flat[:, None] == jnp.arange(count, dtype=jnp.int32)[None, :]).astype(jnp.int32)
    earlier = (jnp.cumsum(table, axis=0) - table).astype(jnp.int32)
    slots = lax.optimization_barrier(jnp.sum(earlier * table, axis=1)).astype(jnp.int32)
    return (flat * capacity + slots).astype(jnp.int32).reshape(ids.shape)

def to_experts(sent):
    members = sent.shape[0]
    return sent.reshape(members, EXPERTS, CAP, D).transpose(1, 0, 2, 3).reshape(EXPERTS, members * CAP, D)

def to_sources(rows):
    members = rows.shape[1] // CAP
    return rows.reshape(EXPERTS, members, CAP, D).transpose(1, 0, 2, 3).reshape(members, EXPERTS * CAP, D)

def one_expert(inputs):
    rows, grads, weight_in, weight_out = inputs
    hidden_pre = jnp.dot(rows, weight_in, preferred_element_type=jnp.float32)
    hidden = jax.nn.gelu(hidden_pre).astype(jnp.bfloat16)
    result = jnp.dot(hidden, weight_out.T, preferred_element_type=jnp.float32).astype(jnp.bfloat16)
    raw = jnp.dot(grads, weight_out, preferred_element_type=jnp.float32)
    grad_hidden = jax.vjp(jax.nn.gelu, hidden_pre)[1](raw)[0].astype(jnp.bfloat16)
    grad_back = jnp.dot(grad_hidden, weight_in.T, preferred_element_type=jnp.float32).astype(jnp.bfloat16)
    part_in = jnp.dot(rows.T, grad_hidden, preferred_element_type=jnp.float32).astype(jnp.bfloat16)
    part_out = jnp.dot(grads.T, hidden, preferred_element_type=jnp.float32).astype(jnp.bfloat16)
    return (result, grad_back, part_in.astype(jnp.float32), part_out.astype(jnp.float32))

def reference(patches, expert_ids, gate_weights, conv_weight, conv_bias, ln_gain, ln_shift, w_in, w_out, grad_mixed):
    members = N_EXPERT
    shaped = partial(front, conv_weight=conv_weight, conv_bias=conv_bias, ln_gain=ln_gain, ln_shift=ln_shift)
    all_slots = jnp.arange(EXPERTS * CAP, dtype=jnp.int32)

    def one_group(carry, inputs):
        patch_g, ids_g, gate_g, cot_g = inputs
        images = patch_g.astype(jnp.float32).reshape(members, IMG_H, IMG_W, D)
        pre, back_front = jax.vjp(shaped, images)
        normed = pre.reshape(members, TOK_DEV, D).astype(jnp.bfloat16)
        ids = ids_g.reshape(members, TOK_DEV, TOP)
        positions = jax.vmap(lambda block: slot_positions(block, CAP, EXPERTS))(ids)
        gates = gate_g.reshape(members, TOK_DEV, TOP)
        hits = (positions[:, None, :, :] == all_slots[None, :, None, None]).astype(jnp.float32)
        select = lax.optimization_barrier(jnp.sum(hits, axis=-1))
        sent = jnp.einsum('mst,mtd->msd', select, normed.astype(jnp.float32)).astype(jnp.bfloat16)
        gate_select = lax.optimization_barrier(jnp.sum(hits * gates[:, None, :, :], axis=-1))
        cot = cot_g.reshape(members, TOK_DEV, D).astype(jnp.float32)
        grad_sent = jnp.einsum('mst,mtd->msd', gate_select, cot, precision=lax.Precision.HIGHEST).astype(jnp.bfloat16)
        outs, grad_back, part_in, part_out = lax.map(one_expert, (to_experts(sent), to_experts(grad_sent), w_in, w_out))
        back = to_sources(outs)
        grad_ret = to_sources(grad_back)
        picked = jax.vmap(lambda table, pos: jnp.take(table, pos.reshape(-1), axis=0))(back, positions)
        picked = picked.reshape(members, TOK_DEV, TOP, D).astype(jnp.float32)
        combined = lax.optimization_barrier(jnp.sum(picked * gates[..., None], axis=2))
        mixed = (patch_g.astype(jnp.float32).reshape(members, TOK_DEV, D) + combined).astype(jnp.bfloat16)
        picked_grad = jax.vmap(lambda table, pos: jnp.take(table, pos.reshape(-1), axis=0))(grad_ret, positions)
        grad_normed = lax.optimization_barrier(jnp.sum(picked_grad.reshape(members, TOK_DEV, TOP, D).astype(jnp.float32), axis=2))
        grad_front = back_front(grad_normed.reshape(members, IMG_H, IMG_W, D))[0]
        grad_input = cot + grad_front.reshape(members, TOK_DEV, D)
        total_in, total_out = carry
        return ((total_in + part_in, total_out + part_out), (mixed.reshape(members * TOK_DEV, D), grad_input.reshape(members * TOK_DEV, D)))
    start = (jnp.zeros((EXPERTS, D, EXP_HID), jnp.float32), jnp.zeros((EXPERTS, D, EXP_HID), jnp.float32))
    inputs = (patches.reshape(N_DP, members * TOK_DEV, D), expert_ids.reshape(N_DP, members * TOK_DEV, TOP), gate_weights.reshape(N_DP, members * TOK_DEV, TOP), grad_mixed.reshape(N_DP, members * TOK_DEV, D))
    (grad_w_in, grad_w_out), (mixed, grad_input) = lax.scan(one_group, start, inputs)
    return (mixed.reshape(TOKENS, D), grad_input.reshape(TOKENS, D), grad_w_in, grad_w_out)
```

```python
import functools

import jax
import jax.numpy as jnp
from jax import lax
from jax.experimental import pallas as pl
from jax.experimental.pallas import tpu as pltpu
from jax.sharding import PartitionSpec as P

KSIZE = 7
HALF = KSIZE // 2
TOP = 2
IMG_W = 16
IMG_H = 8
EPS = 1e-06
EDGE = 8
MESH = pl.DeviceIdType.MESH
BF = jnp.bfloat16
F32 = jnp.float32


def conv_into(pad, weight_ref, out_ref, bias_ref, flip):
    width = out_ref.shape[1]

    def chunk(i, carry):
        lanes = pl.ds(pl.multiple_of(i * 128, 128), 128)
        total = jnp.zeros((IMG_H, IMG_W, 128), F32)
        if bias_ref is not None:
            total = total + bias_ref[0:1, lanes].reshape(1, 1, 128)
        for col in range(KSIZE):
            start = EDGE - HALF + col
            slab = pad[:, start : start + IMG_W, lanes]
            for row in range(KSIZE):
                tap = row * KSIZE + col
                if flip:
                    tap = KSIZE * KSIZE - 1 - tap
                total = total + slab[row : row + IMG_H] * weight_ref[tap : tap + 1, lanes].reshape(
                    1, 1, 128
                )
        out_ref[:, lanes] = total.reshape(IMG_H * IMG_W, 128)
        return carry

    lax.fori_loop(0, width // 128, chunk, 0)


def fill_pad(pad, image):
    pad[...] = jnp.zeros_like(pad)
    pad[HALF : HALF + IMG_H, EDGE : EDGE + IMG_W, :] = image.reshape(IMG_H, IMG_W, image.shape[-1])


def front_body(patches_ref, weight_ref, bias_ref, gain_ref, shift_ref, conv_ref, normed_ref, pad):
    fill_pad(pad, patches_ref[...].astype(F32))
    conv_into(pad, weight_ref, conv_ref, bias_ref, False)
    conv = conv_ref[...]
    centred = conv - jnp.mean(conv, axis=1, keepdims=True)
    spread = jnp.mean(centred * centred, axis=1, keepdims=True)
    normed_ref[...] = (centred * lax.rsqrt(spread + EPS) * gain_ref[...] + shift_ref[...]).astype(
        BF
    )


def back_body(conv_ref, weight_ref, gain_ref, grad_ref, cot_ref, out_ref, pad):
    conv = conv_ref[...]
    centred = conv - jnp.mean(conv, axis=1, keepdims=True)
    spread = jnp.mean(centred * centred, axis=1, keepdims=True)
    scale = lax.rsqrt(spread + EPS)
    unit = centred * scale
    slope = grad_ref[...] * gain_ref[...]
    inner = slope - jnp.mean(slope, axis=1, keepdims=True)
    inner = inner - unit * jnp.mean(slope * unit, axis=1, keepdims=True)
    fill_pad(pad, inner * scale)
    conv_into(pad, weight_ref, out_ref, None, True)
    out_ref[...] += cot_ref[...].astype(F32)


def dot(left, right, dims):
    return lax.dot_general(left, right, (dims, ((), ())), preferred_element_type=F32)


NN = ((1,), (0,))
NT = ((1,), (1,))
TN = ((0,), (0,))


def moe_body(
    n_dp,
    n_exp,
    cap,
    normed_ref,
    cot_ref,
    meta_ref,
    pos_ref,
    gate_ref,
    patches_ref,
    w_in_ref,
    w_out_ref,
    mixed_ref,
    grad_normed_ref,
    gw_in_ref,
    gw_out_ref,
    win,
    wout,
    all_n,
    all_c,
    all_m,
    rows,
    grads,
    slope,
    hidden,
    ghid,
    outs,
    back,
    r_outs,
    r_back,
    part_in,
    part_out,
    r_in,
    r_out,
    w_send,
    w_recv,
    m_send,
    m_recv,
    line_send,
    line_recv,
    twin_send,
    twin_recv,
    ret_send,
    ret_recv,
    g_send,
    g_recv,
):
    dp = lax.axis_index("dp")
    ex = lax.axis_index("expert")
    chips = n_exp // 2
    chip = ex // 2
    core = ex % 2
    depth = w_in_ref.shape[0]
    width = normed_ref.shape[1]
    hid = w_in_ref.shape[1]
    count = n_exp * cap
    tile = 256

    barrier = pltpu.get_barrier_semaphore()
    for i in range(1, n_exp):
        pl.semaphore_signal(
            barrier, inc=1, device_id=(dp, (ex + i) % n_exp), device_id_type=MESH
        )
    for i in range(1, n_dp):
        pl.semaphore_signal(barrier, inc=1, device_id=((dp + i) % n_dp, ex), device_id_type=MESH)
    pl.semaphore_wait(barrier, n_exp - 1 + n_dp - 1)

    def remote(src, dst, send, recv, to):
        return pltpu.make_async_remote_copy(
            src_ref=src, dst_ref=dst, send_sem=send, recv_sem=recv, device_id=to, device_id_type=MESH
        )

    mine = pl.ds(pl.multiple_of(dp * depth, 16), depth)

    metas = []
    for i in range(1, n_exp):
        copy = remote(
            meta_ref, all_m.at[ex], m_send.at[i], m_recv.at[i], (dp, (ex + i) % n_exp)
        )
        copy.start()
        metas.append(copy)

    own = (normed_ref, cot_ref)
    held = (all_n, all_c)

    def line(a, way, k, src_dev, src):
        step = 1 if way == 0 else -1
        return remote(
            src,
            held[a].at[src_dev],
            line_send.at[a, way, k],
            line_recv.at[a, way, k],
            (dp, jnp.clip(ex + 2 * step, core, n_exp - 2 + core)),
        )

    def twin(a, way, k, src_dev, src):
        return remote(
            src,
            held[a].at[src_dev],
            twin_send.at[a, way, k],
            twin_recv.at[a, way, k],
            (dp, 2 * chip + 1 - core),
        )

    def each(way, k):
        if way == 0:
            return chip - k >= 0, chip + 1 < chips, ex - 2 * k
        return chip + k < chips, chip - 1 >= 0, ex + 2 * k

    def send_step(a, k):
        for way in range(2):
            there, ahead, src_dev = each(way, k)
            src_dev = jnp.clip(src_dev, 0, n_exp - 1)
            src = own[a] if k == 0 else held[a].at[src_dev]
            if k > 0:

                @pl.when(there)
                def _(a=a, way=way, k=k, src_dev=src_dev, src=src):
                    line(a, way, k - 1, src_dev, src).wait_recv()
                    twin(a, way, k, src_dev, src).start()

            if k < chips - 1:

                @pl.when(jnp.logical_and(there, ahead))
                def _(a=a, way=way, k=k, src_dev=src_dev, src=src):
                    line(a, way, k, src_dev, src).start()

            if k == 0 and way == 0:
                twin(a, way, k, src_dev, src).start()

    def finish_twins(a):
        for k in range(chips):
            for way in range(2):
                if k == 0 and way == 1:
                    continue
                there, _, src_dev = each(way, k)
                other = jnp.clip(src_dev + 1 - 2 * core, 0, n_exp - 1)

                @pl.when(there)
                def _(a=a, way=way, k=k, other=other):
                    twin(a, way, k, other, held[a].at[other]).wait_recv()

    def finish_sends(a):
        for k in range(chips):
            for way in range(2):
                there, ahead, src_dev = each(way, k)
                src_dev = jnp.clip(src_dev, 0, n_exp - 1)
                if k < chips - 1:

                    @pl.when(jnp.logical_and(there, ahead))
                    def _(a=a, way=way, k=k, src_dev=src_dev):
                        line(a, way, k, src_dev, own[a]).wait_send()

                if k > 0 or way == 0:

                    @pl.when(there)
                    def _(a=a, way=way, k=k, src_dev=src_dev):
                        twin(a, way, k, src_dev, own[a]).wait_send()

    send_step(0, 0)
    weights = []
    for a, (src, dst) in enumerate(((w_in_ref, win), (w_out_ref, wout))):
        for i in range(1, n_dp):
            copy = remote(
                src, dst.at[mine], w_send.at[a, i], w_recv.at[a, i], ((dp + i) % n_dp, ex)
            )
            copy.start()
            weights.append(copy)
    send_step(1, 0)
    win[mine] = w_in_ref[...]
    wout[mine] = w_out_ref[...]
    all_n[ex] = normed_ref[...]
    all_c[ex] = cot_ref[...]
    all_m[ex] = meta_ref[...]
    for k in range(1, chips):
        send_step(0, k)
        send_step(1, k)
    for copy in metas:
        copy.wait()

    tokens = normed_ref.shape[0]
    slots = lax.broadcasted_iota(jnp.int32, (cap, tokens), 0).astype(F32) + (ex * cap).astype(F32)

    def choose(j):
        info = all_m[j]
        first = jnp.where(slots == info[0:1, :], 1.0, 0.0)
        second = jnp.where(slots == info[1:2, :], 1.0, 0.0)
        gate = jnp.sum(first * info[2:3, :] + second * info[3:4, :], axis=1, keepdims=True)
        return (first + second).astype(BF), gate

    finish_twins(0)

    def gather_rows(j, carry):
        select, _ = choose(j)
        at = pl.ds(pl.multiple_of(j * cap, 16), cap)
        rows[at] = dot(select, all_n[j], NN).astype(BF)
        return carry

    lax.fori_loop(0, n_exp, gather_rows, 0)
    for copy in weights[: n_dp - 1]:
        copy.wait()

    def up(n, carry):
        cols = pl.ds(pl.multiple_of(n * tile, tile), tile)
        x = dot(rows[...], win[:, cols], NN)
        c = 0.7978845608028654
        t = jnp.tanh(c * (x + 0.044715 * (x * x * x)))
        half = 0.5 * (1.0 + t)
        hidden[:, cols] = (x * half).astype(BF)
        slope[:, cols] = half + 0.5 * x * (1.0 - t * t) * (c * (1.0 + 3 * 0.044715 * (x * x)))
        return carry

    lax.fori_loop(0, hid // tile, up, 0)

    finish_twins(1)

    def gather_grads(j, carry):
        select, gate = choose(j)
        at = pl.ds(pl.multiple_of(j * cap, 16), cap)
        grads[at] = (dot(select, all_c[j], NN) * gate).astype(BF)
        return carry

    lax.fori_loop(0, n_exp, gather_grads, 0)
    for copy in weights[n_dp - 1 :]:
        copy.wait()

    def down(n, carry):
        cols = pl.ds(pl.multiple_of(n * tile, tile), tile)
        outs[:, cols] = dot(hidden[...], wout[cols, :], NT).astype(BF)
        return carry

    lax.fori_loop(0, width // tile, down, 0)

    my_rows = pl.ds(pl.multiple_of(ex * cap, 16), cap)

    def give_back(a, src, dst):
        copies = []
        for i in range(1, n_exp):
            to = (ex + i) % n_exp
            copy = remote(
                src.at[pl.ds(pl.multiple_of(to * cap, 16), cap)],
                dst.at[my_rows],
                ret_send.at[a, i],
                ret_recv.at[a, i],
                (dp, to),
            )
            copy.start()
            copies.append(copy)
        dst[my_rows] = src[my_rows]
        return copies

    outs_back = give_back(0, outs, r_outs)

    def down_grad(n, carry):
        cols = pl.ds(pl.multiple_of(n * tile, tile), tile)
        ghid[:, cols] = (dot(grads[...], wout[:, cols], NN) * slope[:, cols]).astype(BF)
        return carry

    lax.fori_loop(0, hid // tile, down_grad, 0)

    def up_grad(n, carry):
        cols = pl.ds(pl.multiple_of(n * tile, tile), tile)
        back[:, cols] = dot(ghid[...], win[cols, :], NT).astype(BF)
        return carry

    lax.fori_loop(0, width // tile, up_grad, 0)
    grads_back = give_back(1, back, r_back)

    shares = []

    def weight_grad(a, left, right, part, got):
        for i in range(1, n_dp + 1):
            to = (dp + i) % n_dp
            cols = pl.ds(pl.multiple_of(to * depth, depth), depth) if depth % 128 == 0 else None
            if cols is None:
                break
            part[to] = dot(left[:, cols], right[...], TN).astype(BF)
            if i < n_dp:
                share(a, i, to, part, got)

    def share(a, i, to, part, got):
        copy = remote(part.at[to], got.at[dp], g_send.at[a, i], g_recv.at[a, i], (to, ex))
        copy.start()
        shares.append(copy)

    def weight_grad_wide(a, left, right, part, got):
        def some(n, carry):
            cols = pl.ds(pl.multiple_of(n * tile, tile), tile)
            made = dot(left[:, cols], right[...], TN).astype(BF)
            each_tile = tile // depth
            part[pl.ds(n * each_tile, each_tile)] = made.reshape(each_tile, depth, hid)
            return carry

        lax.fori_loop(0, width // tile, some, 0)
        for i in range(1, n_dp):
            share(a, i, (dp + i) % n_dp, part, got)

    make = weight_grad if depth % 128 == 0 else weight_grad_wide
    make(0, rows, ghid, part_in, r_in)
    make(1, grads, hidden, part_out, r_out)

    wide = lax.broadcasted_iota(jnp.int32, (tokens, count), 1)
    picks = [wide == pos_ref[:, k : k + 1] for k in range(TOP)]
    ones = [jnp.where(pick, 1.0, 0.0).astype(BF) for pick in picks]
    for copy in outs_back:
        copy.wait()
    total = patches_ref[...].astype(F32)
    combined = dot(ones[0], r_outs[...], NN) * gate_ref[:, 0:1]
    for k in range(1, TOP):
        combined = combined + dot(ones[k], r_outs[...], NN) * gate_ref[:, k : k + 1]
    mixed_ref[...] = (total + combined).astype(BF)
    for copy in grads_back:
        copy.wait()
    both = ones[0]
    for k in range(1, TOP):
        both = both + ones[k]
    grad_normed_ref[...] = dot(both, r_back[...], NN)

    for copy in shares:
        copy.wait()
    for part, got, out in ((part_in, r_in, gw_in_ref), (part_out, r_out, gw_out_ref)):
        value = part[dp].astype(F32)
        for i in range(1, n_dp):
            value = value + got[(dp + i) % n_dp].astype(F32)
        out[...] = value
    finish_sends(0)
    finish_sends(1)


def local(
    patches,
    expert_ids,
    gate_weights,
    conv_weight,
    conv_bias,
    ln_gain,
    ln_shift,
    w_in,
    w_out,
    grad_mixed,
):
    tokens, width = patches.shape
    depth, hid = w_in.shape[1:]
    n_exp = lax.axis_size("expert")
    n_dp = lax.axis_size("dp")
    cap = 4 * tokens // n_exp
    count = n_exp * cap
    bias, gain, shift = conv_bias[None], ln_gain[None], ln_shift[None]
    vmem = pl.BlockSpec(memory_space=pltpu.VMEM)
    pad = pltpu.VMEM((IMG_H + 2 * HALF, IMG_W + 2 * EDGE, width), F32)
    conv, normed = pl.pallas_call(
        front_body,
        out_shape=(
            jax.ShapeDtypeStruct((tokens, width), F32),
            jax.ShapeDtypeStruct((tokens, width), BF),
        ),
        in_specs=[vmem] * 5,
        out_specs=(vmem, vmem),
        scratch_shapes=[pad],
        compiler_params=pltpu.CompilerParams(vmem_limit_bytes=24 << 20),
    )(patches, conv_weight, bias, gain, shift)

    flat = expert_ids.reshape(-1)
    table = (flat[:, None] == jnp.arange(n_exp, dtype=jnp.int32)[None, :]).astype(BF)
    pairs = TOP * tokens
    before = jnp.tril(jnp.ones((pairs, pairs), BF), -1)
    earlier = jnp.dot(before, table, preferred_element_type=F32)
    slots = jnp.sum(earlier * table.astype(F32), axis=1).astype(jnp.int32)
    positions = (flat * cap + slots).reshape(tokens, TOP)
    meta = jnp.concatenate(
        [positions.astype(F32).T, gate_weights.T, jnp.zeros((8 - 2 * TOP, tokens), F32)], axis=0
    )

    dma = pltpu.SemaphoreType.DMA
    chips = n_exp // 2
    mixed, grad_normed, gw_in, gw_out = pl.pallas_call(
        functools.partial(moe_body, n_dp, n_exp, cap),
        out_shape=(
            jax.ShapeDtypeStruct((tokens, width), BF),
            jax.ShapeDtypeStruct((tokens, width), F32),
            jax.ShapeDtypeStruct((depth, hid), F32),
            jax.ShapeDtypeStruct((depth, hid), F32),
        ),
        in_specs=[vmem] * 8,
        out_specs=(vmem,) * 4,
        scratch_shapes=[
            pltpu.VMEM((width, hid), BF),
            pltpu.VMEM((width, hid), BF),
            pltpu.VMEM((n_exp, tokens, width), BF),
            pltpu.VMEM((n_exp, tokens, width), BF),
            pltpu.VMEM((n_exp, 8, tokens), F32),
            pltpu.VMEM((count, width), BF),
            pltpu.VMEM((count, width), BF),
            pltpu.VMEM((count, hid), F32),
            pltpu.VMEM((count, hid), BF),
            pltpu.VMEM((count, hid), BF),
            pltpu.VMEM((count, width), BF),
            pltpu.VMEM((count, width), BF),
            pltpu.VMEM((count, width), BF),
            pltpu.VMEM((count, width), BF),
            pltpu.VMEM((n_dp, depth, hid), BF),
            pltpu.VMEM((n_dp, depth, hid), BF),
            pltpu.VMEM((n_dp, depth, hid), BF),
            pltpu.VMEM((n_dp, depth, hid), BF),
            dma((2, n_dp)),
            dma((2, n_dp)),
            dma((n_exp,)),
            dma((n_exp,)),
            dma((2, 2, chips)),
            dma((2, 2, chips)),
            dma((2, 2, chips)),
            dma((2, 2, chips)),
            dma((2, n_exp)),
            dma((2, n_exp)),
            dma((2, n_dp)),
            dma((2, n_dp)),
        ],
        compiler_params=pltpu.CompilerParams(
            collective_id=0, has_side_effects=True, vmem_limit_bytes=56 << 20
        ),
    )(normed, grad_mixed, meta, positions, gate_weights, patches, w_in[0], w_out[0])

    grad_input = pl.pallas_call(
        back_body,
        out_shape=jax.ShapeDtypeStruct((tokens, width), F32),
        in_specs=[vmem] * 5,
        out_specs=vmem,
        scratch_shapes=[pad],
        compiler_params=pltpu.CompilerParams(vmem_limit_bytes=24 << 20),
    )(conv, conv_weight, gain, grad_normed, grad_mixed)
    return mixed, grad_input, gw_in[None], gw_out[None]


def solution(mesh):
    rows = P(("dp", "expert"), None)
    split = P("expert", "dp", None)
    return jax.shard_map(
        local,
        mesh=mesh,
        in_specs=(rows, rows, rows, P(), P(), P(), P(), split, split, rows),
        out_specs=(rows, rows, split, split),
        check_vma=False,
    )
```

```python
import functools

import jax
import jax.numpy as jnp
from jax import lax
from jax.experimental import pallas as pl
from jax.experimental.pallas import tpu as pltpu
from jax.sharding import PartitionSpec as P

KSIZE = 7
HALF = KSIZE // 2
TOP = 2
IMG_W = 16
IMG_H = 8
EPS = 1e-06
EDGE = 8
MESH = pl.DeviceIdType.MESH
BF = jnp.bfloat16
F32 = jnp.float32


def conv_into(pad, weight_ref, out_ref, bias_ref, flip):
    width = out_ref.shape[1]

    def chunk(i, carry):
        lanes = pl.ds(pl.multiple_of(i * 128, 128), 128)
        total = jnp.zeros((IMG_H, IMG_W, 128), F32)
        if bias_ref is not None:
            total = total + bias_ref[0:1, lanes].reshape(1, 1, 128)
        for col in range(KSIZE):
            start = EDGE - HALF + col
            slab = pad[:, start : start + IMG_W, lanes]
            for row in range(KSIZE):
                tap = row * KSIZE + col
                if flip:
                    tap = KSIZE * KSIZE - 1 - tap
                total = total + slab[row : row + IMG_H] * weight_ref[tap : tap + 1, lanes].reshape(
                    1, 1, 128
                )
        out_ref[:, lanes] = total.reshape(IMG_H * IMG_W, 128)
        return carry

    lax.fori_loop(0, width // 128, chunk, 0)


def fill_pad(pad, image):
    pad[...] = jnp.zeros_like(pad)
    pad[HALF : HALF + IMG_H, EDGE : EDGE + IMG_W, :] = image.reshape(IMG_H, IMG_W, image.shape[-1])


def normalise(conv):
    centred = conv - jnp.mean(conv, axis=1, keepdims=True)
    spread = jnp.mean(centred * centred, axis=1, keepdims=True)
    scale = lax.rsqrt(spread + EPS)
    return centred * scale, scale


def dot(left, right, dims):
    return lax.dot_general(left, right, (dims, ((), ())), preferred_element_type=F32)


NN = ((1,), (0,))
NT = ((1,), (1,))
TN = ((0,), (0,))


def moe_body(
    n_dp,
    n_exp,
    cap,
    patches_ref,
    ids_ref,
    gate_ref,
    taps_ref,
    bias_ref,
    gain_ref,
    shift_ref,
    w_in_ref,
    w_out_ref,
    cot_ref,
    mixed_ref,
    grad_ref,
    gw_in_ref,
    gw_out_ref,
    pad,
    conv,
    normed,
    meta,
    flip,
    win,
    wout,
    all_n,
    all_c,
    all_m,
    rows,
    grads,
    slope,
    hidden,
    ghid,
    outs,
    back,
    r_outs,
    r_back,
    part_in,
    part_out,
    first_got,
    staged,
    second_got,
    w_send,
    w_recv,
    m_send,
    m_recv,
    line_send,
    line_recv,
    twin_send,
    twin_recv,
    ret_send,
    ret_recv,
    g_send,
    g_recv,
    h_send,
    h_recv,
):
    dp = lax.axis_index("dp")
    ex = lax.axis_index("expert")
    chips = n_exp // 2
    chip = ex // 2
    core = ex % 2
    depth, hid = w_in_ref.shape
    tokens, width = patches_ref.shape
    count = n_exp * cap
    tile = 256
    sides = grid_of(n_dp)
    spot = (dp // sides[1], dp % sides[1])
    half = depth // 2

    def dp_at(first, second, turned):
        return second * sides[1] + first if turned else first * sides[1] + second

    barrier = pltpu.get_barrier_semaphore()
    for i in range(1, n_exp):
        pl.semaphore_signal(
            barrier, inc=1, device_id=(dp, (ex + i) % n_exp), device_id_type=MESH
        )
    for i in range(1, n_dp):
        pl.semaphore_signal(barrier, inc=1, device_id=((dp + i) % n_dp, ex), device_id_type=MESH)
    pl.semaphore_wait(barrier, n_exp - 1 + n_dp - 1)

    def remote(src, dst, send, recv, to):
        return pltpu.make_async_remote_copy(
            src_ref=src, dst_ref=dst, send_sem=send, recv_sem=recv, device_id=to, device_id_type=MESH
        )

    full = (win, wout)
    shard = (w_in_ref, w_out_ref)
    started = []

    def sides_of(h):
        return sides[1 - h], spot[1 - h], sides[h], spot[h]

    def half_at(who, h):
        return pl.ds(pl.multiple_of(who * depth + h * half, 16), half)

    def weight_copy(a, h, i, j, own):
        n_one, one, n_two, two = sides_of(h)
        origin = dp_at((one - i) % n_one, two, h == 0)
        if j == 0:
            to = dp_at((one + i) % n_one, two, h == 0)
            origin = dp
        else:
            to = dp_at(one, (two + j) % n_two, h == 0)
        src = shard[a].at[pl.ds(h * half, half)] if own else full[a].at[half_at(origin, h)]
        return remote(
            src,
            full[a].at[half_at(origin, h)],
            w_send.at[a, h, i, j],
            w_recv.at[a, h, i, j],
            (to, ex),
        )

    def weights_first(a):
        for h in range(2):
            n_one, _, n_two, _ = sides_of(h)
            for i in range(1, n_one):
                copy = weight_copy(a, h, i, 0, True)
                copy.start()
                started.append(copy)
        for h in range(2):
            n_one, _, n_two, _ = sides_of(h)
            for j in range(1, n_two):
                copy = weight_copy(a, h, 0, j, True)
                copy.start()
                started.append(copy)

    def weights_on(a):
        for h in range(2):
            n_one, _, n_two, _ = sides_of(h)
            for i in range(1, n_one):
                weight_copy(a, h, i, 0, True).wait_recv()
                for j in range(1, n_two):
                    copy = weight_copy(a, h, i, j, False)
                    copy.start()
                    started.append(copy)

    def weights_done(a):
        for h in range(2):
            n_one, _, n_two, _ = sides_of(h)
            for i in range(n_one):
                for j in range(1, n_two):
                    weight_copy(a, h, i, j, i == 0).wait_recv()

    own = (normed, cot_ref)
    held = (all_n, all_c)

    def line(a, way, k, src_dev, src):
        step = 1 if way == 0 else -1
        return remote(
            src,
            held[a].at[src_dev],
            line_send.at[a, way, k],
            line_recv.at[a, way, k],
            (dp, jnp.clip(ex + 2 * step, core, n_exp - 2 + core)),
        )

    def twin(a, way, k, src_dev, src):
        return remote(
            src,
            held[a].at[src_dev],
            twin_send.at[a, way, k],
            twin_recv.at[a, way, k],
            (dp, 2 * chip + 1 - core),
        )

    def each(way, k):
        if way == 0:
            return chip - k >= 0, chip + 1 < chips, ex - 2 * k
        return chip + k < chips, chip - 1 >= 0, ex + 2 * k

    def send_step(a, k):
        for way in range(2):
            there, ahead, src_dev = each(way, k)
            src_dev = jnp.clip(src_dev, 0, n_exp - 1)
            src = own[a] if k == 0 else held[a].at[src_dev]
            if k > 0:

                @pl.when(there)
                def _(a=a, way=way, k=k, src_dev=src_dev, src=src):
                    line(a, way, k - 1, src_dev, src).wait_recv()

            if k < chips - 1:

                @pl.when(jnp.logical_and(there, ahead))
                def _(a=a, way=way, k=k, src_dev=src_dev, src=src):
                    line(a, way, k, src_dev, src).start()

            if k > 0:

                @pl.when(there)
                def _(a=a, way=way, k=k, src_dev=src_dev, src=src):
                    twin(a, way, k, src_dev, src).start()

            elif way == 1:
                twin(a, 0, k, src_dev, src).start()

    def finish_twins(a):
        for k in range(chips):
            for way in range(2):
                if k == 0 and way == 1:
                    continue
                there, _, src_dev = each(way, k)
                other = jnp.clip(src_dev + 1 - 2 * core, 0, n_exp - 1)

                @pl.when(there)
                def _(a=a, way=way, k=k, other=other):
                    twin(a, way, k, other, held[a].at[other]).wait_recv()

    def finish_sends(a):
        for k in range(chips):
            for way in range(2):
                there, ahead, src_dev = each(way, k)
                src_dev = jnp.clip(src_dev, 0, n_exp - 1)
                if k < chips - 1:

                    @pl.when(jnp.logical_and(there, ahead))
                    def _(a=a, way=way, k=k, src_dev=src_dev):
                        line(a, way, k, src_dev, own[a]).wait_send()

                if k > 0 or way == 0:

                    @pl.when(there)
                    def _(a=a, way=way, k=k, src_dev=src_dev):
                        twin(a, way, k, src_dev, own[a]).wait_send()

    send_step(1, 0)
    weights_first(0)
    weights_first(1)

    fill_pad(pad, patches_ref[...].astype(F32))
    conv_into(pad, taps_ref, conv, bias_ref, False)
    unit, _ = normalise(conv[...])
    normed[...] = (unit * gain_ref[...] + shift_ref[...]).astype(BF)
    send_step(0, 0)

    flip[...] = jnp.zeros_like(flip)
    flip[:, 0:TOP] = ids_ref[...].astype(F32)
    flip[:, TOP : 2 * TOP] = gate_ref[...]
    turned = jnp.transpose(flip[...])
    names = lax.broadcasted_iota(jnp.int32, (n_exp, tokens), 0).astype(F32)
    named = [jnp.where(names == turned[k : k + 1, :], 1.0, 0.0) for k in range(TOP)]
    before = lax.broadcasted_iota(jnp.int32, (tokens, tokens), 0) < lax.broadcasted_iota(
        jnp.int32, (tokens, tokens), 1
    )
    table = named[0]
    for k in range(1, TOP):
        table = table + named[k]
    rank = dot(table.astype(BF), jnp.where(before, 1.0, 0.0).astype(BF), NN)
    places = [
        turned[k : k + 1, :] * cap + jnp.sum(named[k] * rank, axis=0, keepdims=True)
        for k in range(TOP)
    ]
    meta[...] = jnp.zeros_like(meta)
    for k in range(TOP):
        meta[k : k + 1, :] = places[k]
        meta[TOP + k : TOP + k + 1, :] = turned[TOP + k : TOP + k + 1, :]
    metas = []
    for i in range(1, n_exp):
        copy = remote(meta, all_m.at[ex], m_send.at[i], m_recv.at[i], (dp, (ex + i) % n_exp))
        copy.start()
        metas.append(copy)

    mine = pl.ds(pl.multiple_of(dp * depth, 16), depth)
    win[mine] = w_in_ref[...]
    wout[mine] = w_out_ref[...]
    all_n[ex] = normed[...]
    all_c[ex] = cot_ref[...]
    all_m[ex] = meta[...]
    for k in range(1, max(chips, 2)):
        if k < chips:
            send_step(1, k)
        if k == 1:
            weights_on(0)
        if k < chips:
            send_step(0, k)
        if k == 1:
            weights_on(1)
    for copy in metas:
        copy.wait()

    slots = lax.broadcasted_iota(jnp.int32, (cap, tokens), 0).astype(F32) + (ex * cap).astype(F32)

    def choose(j):
        info = all_m[j]
        hits = [jnp.where(slots == info[k : k + 1, :], 1.0, 0.0) for k in range(TOP)]
        weighed = hits[0] * info[TOP : TOP + 1, :]
        for k in range(1, TOP):
            weighed = weighed + hits[k] * info[TOP + k : TOP + k + 1, :]
        select = hits[0]
        for k in range(1, TOP):
            select = select + hits[k]
        return select.astype(BF), jnp.sum(weighed, axis=1, keepdims=True)

    finish_twins(1)

    def gather_grads(j, carry):
        select, gate = choose(j)
        at = pl.ds(pl.multiple_of(j * cap, 16), cap)
        grads[at] = (dot(select, all_c[j], NN) * gate).astype(BF)
        return carry

    lax.fori_loop(0, n_exp, gather_grads, 0)
    finish_twins(0)

    def gather_rows(j, carry):
        select, _ = choose(j)
        at = pl.ds(pl.multiple_of(j * cap, 16), cap)
        rows[at] = dot(select, all_n[j], NN).astype(BF)
        return carry

    lax.fori_loop(0, n_exp, gather_rows, 0)
    weights_done(0)

    def up(n, carry):
        cols = pl.ds(pl.multiple_of(n * tile, tile), tile)
        x = dot(rows[...], win[:, cols], NN)
        c = 0.7978845608028654
        t = jnp.tanh(c * (x + 0.044715 * (x * x * x)))
        side = 0.5 * (1.0 + t)
        hidden[:, cols] = (x * side).astype(BF)
        slope[:, cols] = side + 0.5 * x * (1.0 - t * t) * (c * (1.0 + 3 * 0.044715 * (x * x)))
        return carry

    lax.fori_loop(0, hid // tile, up, 0)

    parts = (part_in, part_out)
    shares = []

    def first_share(a, h, j, i):
        n_one, one, n_two, two = sides_of(h)
        whose = dp_at(i, (two + j) % n_two, h == 0)
        to = dp_at(one, (two + j) % n_two, h == 0)
        return remote(
            parts[a].at[whose, pl.ds(h * half, half)],
            first_got.at[a, h, j - 1, i],
            g_send.at[a, h, j, i],
            g_recv.at[a, h, j, i],
            (to, ex),
        )

    def weight_grad(a, left, right):
        part = parts[a]
        if depth % 128 == 0:
            for i in range(1, n_dp + 1):
                to = (dp + i) % n_dp
                cols = pl.ds(pl.multiple_of(to * depth, depth), depth)
                part[to] = dot(left[:, cols], right[...], TN).astype(BF)
        else:

            def some(n, carry):
                cols = pl.ds(pl.multiple_of(n * tile, tile), tile)
                made = dot(left[:, cols], right[...], TN).astype(BF)
                many = tile // depth
                part[pl.ds(n * many, many)] = made.reshape(many, depth, hid)
                return carry

            lax.fori_loop(0, width // tile, some, 0)
        for h in range(2):
            n_one, _, n_two, _ = sides_of(h)
            for j in range(1, n_two):
                for i in range(n_one):
                    copy = first_share(a, h, j, i)
                    copy.start()
                    shares.append(copy)

    def met(a, h, place):
        n_one, one, n_two, two = sides_of(h)
        value = parts[a][dp_at(place, two, h == 0), pl.ds(h * half, half)].astype(F32)
        for j in range(1, n_two):
            value = value + first_got[a, h, j - 1, place].astype(F32)
        return value

    def second_shares(a):
        for h in range(2):
            n_one, one, n_two, two = sides_of(h)
            for j in range(1, n_two):
                for i in range(n_one):
                    first_share(a, h, j, i).wait_recv()
            for i in range(1, n_one):
                place = (one + i) % n_one
                staged[a, h, i - 1] = met(a, h, place).astype(BF)
                copy = remote(
                    staged.at[a, h, i - 1],
                    second_got.at[a, h, i - 1],
                    h_send.at[a, h, i],
                    h_recv.at[a, h, i],
                    (dp_at(place, two, h == 0), ex),
                )
                copy.start()
                seconds[a].append(copy)

    seconds = ([], [])

    def weight_sum(a, out):
        for copy in seconds[a]:
            copy.wait()
        for h in range(2):
            n_one, one, n_two, two = sides_of(h)
            value = met(a, h, one)
            for i in range(1, n_one):
                value = value + second_got[a, h, i - 1].astype(F32)
            out[pl.ds(h * half, half)] = value

    weights_done(1)

    def down(n, carry):
        cols = pl.ds(pl.multiple_of(n * tile, tile), tile)
        outs[:, cols] = dot(hidden[...], wout[cols, :], NT).astype(BF)
        return carry

    lax.fori_loop(0, width // tile, down, 0)

    my_rows = pl.ds(pl.multiple_of(ex * cap, 16), cap)

    def give_back(a, src, dst):
        copies = []
        for i in range(1, n_exp):
            to = (ex + i) % n_exp
            copy = remote(
                src.at[pl.ds(pl.multiple_of(to * cap, 16), cap)],
                dst.at[my_rows],
                ret_send.at[a, i],
                ret_recv.at[a, i],
                (dp, to),
            )
            copy.start()
            copies.append(copy)
        dst[my_rows] = src[my_rows]
        return copies

    outs_back = give_back(0, outs, r_outs)
    weight_grad(1, grads, hidden)

    def down_grad(n, carry):
        cols = pl.ds(pl.multiple_of(n * tile, tile), tile)
        ghid[:, cols] = (dot(grads[...], wout[:, cols], NN) * slope[:, cols]).astype(BF)
        return carry

    lax.fori_loop(0, hid // tile, down_grad, 0)

    def up_grad(n, carry):
        cols = pl.ds(pl.multiple_of(n * tile, tile), tile)
        back[:, cols] = dot(ghid[...], win[cols, :], NT).astype(BF)
        return carry

    lax.fori_loop(0, width // tile, up_grad, 0)
    grads_back = give_back(1, back, r_back)
    weight_grad(0, rows, ghid)
    second_shares(1)

    tall = lax.broadcasted_iota(jnp.int32, (count, tokens), 0).astype(F32)
    ones = [jnp.where(tall == meta[k : k + 1, :], 1.0, 0.0).astype(BF) for k in range(TOP)]
    for copy in outs_back:
        copy.wait()
    combined = dot(ones[0], r_outs[...], TN) * gate_ref[:, 0:1]
    for k in range(1, TOP):
        combined = combined + dot(ones[k], r_outs[...], TN) * gate_ref[:, k : k + 1]
    mixed_ref[...] = (patches_ref[...].astype(F32) + combined).astype(BF)
    second_shares(0)

    for copy in grads_back:
        copy.wait()
    both = ones[0]
    for k in range(1, TOP):
        both = both + ones[k]
    unit, scale = normalise(conv[...])
    lean = dot(both, r_back[...], TN) * gain_ref[...]
    inner = lean - jnp.mean(lean, axis=1, keepdims=True)
    inner = inner - unit * jnp.mean(lean * unit, axis=1, keepdims=True)
    fill_pad(pad, inner * scale)
    conv_into(pad, taps_ref, grad_ref, None, True)
    grad_ref[...] += cot_ref[...].astype(F32)

    weight_sum(1, gw_out_ref)
    weight_sum(0, gw_in_ref)
    for copy in started + shares:
        copy.wait_send()
    finish_sends(0)
    finish_sends(1)


def grid_of(n_dp):
    side = max(i for i in range(1, n_dp + 1) if n_dp % i == 0 and i * i <= n_dp)
    return side, n_dp // side


def local(
    patches,
    expert_ids,
    gate_weights,
    conv_weight,
    conv_bias,
    ln_gain,
    ln_shift,
    w_in,
    w_out,
    grad_mixed,
):
    tokens, width = patches.shape
    depth, hid = w_in.shape[1:]
    n_exp = lax.axis_size("expert")
    n_dp = lax.axis_size("dp")
    cap = 4 * tokens // n_exp
    count = n_exp * cap
    vmem = pl.BlockSpec(memory_space=pltpu.VMEM)
    dma = pltpu.SemaphoreType.DMA
    chips = n_exp // 2
    long = max(grid_of(n_dp))
    more = max(long - 1, 1)
    half = depth // 2
    mixed, grad_input, gw_in, gw_out = pl.pallas_call(
        functools.partial(moe_body, n_dp, n_exp, cap),
        out_shape=(
            jax.ShapeDtypeStruct((tokens, width), BF),
            jax.ShapeDtypeStruct((tokens, width), F32),
            jax.ShapeDtypeStruct((depth, hid), F32),
            jax.ShapeDtypeStruct((depth, hid), F32),
        ),
        in_specs=[vmem] * 10,
        out_specs=(vmem,) * 4,
        scratch_shapes=[
            pltpu.VMEM((IMG_H + 2 * HALF, IMG_W + 2 * EDGE, width), F32),
            pltpu.VMEM((tokens, width), F32),
            pltpu.VMEM((tokens, width), BF),
            pltpu.VMEM((8, tokens), F32),
            pltpu.VMEM((tokens, 128), F32),
            pltpu.VMEM((width, hid), BF),
            pltpu.VMEM((width, hid), BF),
            pltpu.VMEM((n_exp, tokens, width), BF),
            pltpu.VMEM((n_exp, tokens, width), BF),
            pltpu.VMEM((n_exp, 8, tokens), F32),
            pltpu.VMEM((count, width), BF),
            pltpu.VMEM((count, width), BF),
            pltpu.VMEM((count, hid), F32),
            pltpu.VMEM((count, hid), BF),
            pltpu.VMEM((count, hid), BF),
            pltpu.VMEM((count, width), BF),
            pltpu.VMEM((count, width), BF),
            pltpu.VMEM((count, width), BF),
            pltpu.VMEM((count, width), BF),
            pltpu.VMEM((n_dp, depth, hid), BF),
            pltpu.VMEM((n_dp, depth, hid), BF),
            pltpu.VMEM((2, 2, more, long, half, hid), BF),
            pltpu.VMEM((2, 2, more, half, hid), BF),
            pltpu.VMEM((2, 2, more, half, hid), BF),
            dma((2, 2, long, long)),
            dma((2, 2, long, long)),
            dma((n_exp,)),
            dma((n_exp,)),
            dma((2, 2, chips)),
            dma((2, 2, chips)),
            dma((2, 2, chips)),
            dma((2, 2, chips)),
            dma((2, n_exp)),
            dma((2, n_exp)),
            dma((2, 2, long, long)),
            dma((2, 2, long, long)),
            dma((2, 2, long)),
            dma((2, 2, long)),
        ],
        compiler_params=pltpu.CompilerParams(
            collective_id=0, has_side_effects=True, vmem_limit_bytes=58 << 20
        ),
    )(
        patches,
        expert_ids,
        gate_weights,
        conv_weight,
        conv_bias[None],
        ln_gain[None],
        ln_shift[None],
        w_in[0],
        w_out[0],
        grad_mixed,
    )
    return mixed, grad_input, gw_in[None], gw_out[None]


def solution(mesh):
    rows = P(("dp", "expert"), None)
    split = P("expert", "dp", None)
    return jax.shard_map(
        local,
        mesh=mesh,
        in_specs=(rows, rows, rows, P(), P(), P(), P(), split, split, rows),
        out_specs=(rows, rows, split, split),
        check_vma=False,
    )
```

```python
import functools

import jax
import jax.numpy as jnp
from jax import lax
from jax.experimental import pallas as pl
from jax.experimental.pallas import tpu as pltpu
from jax.sharding import PartitionSpec as P

KSIZE = 7
HALF = KSIZE // 2
TOP = 2
IMG_W = 16
IMG_H = 8
EPS = 1e-06
EDGE = 8
MESH = pl.DeviceIdType.MESH
BF = jnp.bfloat16
F32 = jnp.float32


def conv_into(pad, weight_ref, out_ref, bias_ref, flip):
    width = out_ref.shape[1]

    def chunk(i, carry):
        lanes = pl.ds(pl.multiple_of(i * 128, 128), 128)
        total = jnp.zeros((IMG_H, IMG_W, 128), F32)
        if bias_ref is not None:
            total = total + bias_ref[0:1, lanes].reshape(1, 1, 128)
        for col in range(KSIZE):
            start = EDGE - HALF + col
            slab = pad[:, start : start + IMG_W, lanes]
            for row in range(KSIZE):
                tap = row * KSIZE + col
                if flip:
                    tap = KSIZE * KSIZE - 1 - tap
                total = total + slab[row : row + IMG_H] * weight_ref[tap : tap + 1, lanes].reshape(
                    1, 1, 128
                )
        out_ref[:, lanes] = total.reshape(IMG_H * IMG_W, 128)
        return carry

    lax.fori_loop(0, width // 128, chunk, 0)


def fill_pad(pad, image):
    pad[...] = jnp.zeros_like(pad)
    pad[HALF : HALF + IMG_H, EDGE : EDGE + IMG_W, :] = image.reshape(IMG_H, IMG_W, image.shape[-1])


def normalise(conv):
    centred = conv - jnp.mean(conv, axis=1, keepdims=True)
    spread = jnp.mean(centred * centred, axis=1, keepdims=True)
    scale = lax.rsqrt(spread + EPS)
    return centred * scale, scale


def dot(left, right, dims):
    return lax.dot_general(left, right, (dims, ((), ())), preferred_element_type=F32)


NN = ((1,), (0,))
NT = ((1,), (1,))
TN = ((0,), (0,))


def moe_body(
    n_dp,
    n_exp,
    cap,
    patches_ref,
    ids_ref,
    gate_ref,
    taps_ref,
    bias_ref,
    gain_ref,
    shift_ref,
    w_in_ref,
    w_out_ref,
    cot_ref,
    mixed_ref,
    grad_ref,
    gw_in_ref,
    gw_out_ref,
    pad,
    conv,
    normed,
    flip,
    sent_n,
    sent_g,
    picked,
    single,
    win,
    wout,
    rows,
    grads,
    slope,
    hidden,
    ghid,
    outs,
    back,
    r_outs,
    r_back,
    part_in,
    part_out,
    first_got,
    staged,
    second_got,
    w_send,
    w_recv,
    ret_send,
    ret_recv,
    g_send,
    g_recv,
    h_send,
    h_recv,
):
    dp = lax.axis_index("dp")
    ex = lax.axis_index("expert")
    depth, hid = w_in_ref.shape
    tokens, width = patches_ref.shape
    count = n_exp * cap
    tile = 256
    sides = grid_of(n_dp)
    spot = (dp // sides[1], dp % sides[1])
    half = depth // 2

    def dp_at(first, second, turned):
        return second * sides[1] + first if turned else first * sides[1] + second

    barrier = pltpu.get_barrier_semaphore()
    for i in range(1, n_exp):
        pl.semaphore_signal(
            barrier, inc=1, device_id=(dp, (ex + i) % n_exp), device_id_type=MESH
        )
    for i in range(1, n_dp):
        pl.semaphore_signal(barrier, inc=1, device_id=((dp + i) % n_dp, ex), device_id_type=MESH)

    def remote(src, dst, send, recv, to):
        return pltpu.make_async_remote_copy(
            src_ref=src, dst_ref=dst, send_sem=send, recv_sem=recv, device_id=to, device_id_type=MESH
        )

    full = (win, wout)
    shard = (w_in_ref, w_out_ref)
    started = []

    def sides_of(h):
        return sides[1 - h], spot[1 - h], sides[h], spot[h]

    def half_at(who, h):
        return pl.ds(pl.multiple_of(who * depth + h * half, 16), half)

    def weight_copy(a, h, i, j, own):
        n_one, one, n_two, two = sides_of(h)
        origin = dp_at((one - i) % n_one, two, h == 0)
        if j == 0:
            to = dp_at((one + i) % n_one, two, h == 0)
            origin = dp
        else:
            to = dp_at(one, (two + j) % n_two, h == 0)
        src = shard[a].at[pl.ds(h * half, half)] if own else full[a].at[half_at(origin, h)]
        return remote(
            src,
            full[a].at[half_at(origin, h)],
            w_send.at[a, h, i, j],
            w_recv.at[a, h, i, j],
            (to, ex),
        )

    def weights_first(a):
        for h in range(2):
            n_one, _, n_two, _ = sides_of(h)
            for i in range(1, n_one):
                copy = weight_copy(a, h, i, 0, True)
                copy.start()
                started.append(copy)
        for h in range(2):
            n_one, _, n_two, _ = sides_of(h)
            for j in range(1, n_two):
                copy = weight_copy(a, h, 0, j, True)
                copy.start()
                started.append(copy)

    def weights_on(a):
        for h in range(2):
            n_one, _, n_two, _ = sides_of(h)
            for i in range(1, n_one):
                weight_copy(a, h, i, 0, True).wait_recv()
                for j in range(1, n_two):
                    copy = weight_copy(a, h, i, j, False)
                    copy.start()
                    started.append(copy)

    def weights_done(a):
        for h in range(2):
            n_one, _, n_two, _ = sides_of(h)
            for i in range(n_one):
                for j in range(1, n_two):
                    weight_copy(a, h, i, j, i == 0).wait_recv()

    my_rows = pl.ds(pl.multiple_of(ex * cap, 16), cap)

    def exchange(a, src, dst):
        copies = []
        for i in range(1, n_exp):
            to = (ex + i) % n_exp
            copy = remote(
                src.at[pl.ds(pl.multiple_of(to * cap, 16), cap)],
                dst.at[my_rows],
                ret_send.at[a, i],
                ret_recv.at[a, i],
                (dp, to),
            )
            copy.start()
            copies.append(copy)
        dst[my_rows] = src[my_rows]
        return copies

    flip[...] = jnp.zeros_like(flip)
    flip[:, 0:TOP] = ids_ref[...].astype(F32)
    flip[:, TOP : 2 * TOP] = gate_ref[...]
    turned = jnp.transpose(flip[...])
    names = lax.broadcasted_iota(jnp.int32, (n_exp, tokens), 0).astype(F32)
    named = [jnp.where(names == turned[k : k + 1, :], 1.0, 0.0) for k in range(TOP)]
    before = lax.broadcasted_iota(jnp.int32, (tokens, tokens), 0) < lax.broadcasted_iota(
        jnp.int32, (tokens, tokens), 1
    )
    table = named[0]
    for k in range(1, TOP):
        table = table + named[k]
    rank = dot(table.astype(BF), jnp.where(before, 1.0, 0.0).astype(BF), NN)
    places = [
        turned[k : k + 1, :] * cap + jnp.sum(named[k] * rank, axis=0, keepdims=True)
        for k in range(TOP)
    ]
    tall = lax.broadcasted_iota(jnp.int32, (count, tokens), 0).astype(F32)
    hits = [jnp.where(tall == places[k], 1.0, 0.0) for k in range(TOP)]
    ones = [hit.astype(BF) for hit in hits]
    weighed = hits[0] * turned[TOP : TOP + 1, :]
    for k in range(1, TOP):
        weighed = weighed + hits[k] * turned[TOP + k : TOP + k + 1, :]
    gates = jnp.sum(weighed, axis=1, keepdims=True)
    both_hits = hits[0]
    for k in range(1, TOP):
        both_hits = both_hits + hits[k]
    picked[...] = both_hits.astype(BF)
    for k in range(TOP):
        single[k] = ones[k]

    pl.semaphore_wait(barrier, n_exp - 1 + n_dp - 1)
    weights_first(0)
    sent_g[...] = (dot(picked[...], cot_ref[...], NN) * gates).astype(BF)
    grads_there = exchange(1, sent_g, grads)
    weights_first(1)

    fill_pad(pad, patches_ref[...].astype(F32))
    conv_into(pad, taps_ref, conv, bias_ref, False)
    unit, _ = normalise(conv[...])
    normed[...] = (unit * gain_ref[...] + shift_ref[...]).astype(BF)
    sent_n[...] = dot(picked[...], normed[...], NN).astype(BF)
    rows_there = exchange(0, sent_n, rows)

    mine = pl.ds(pl.multiple_of(dp * depth, 16), depth)
    win[mine] = w_in_ref[...]
    wout[mine] = w_out_ref[...]
    weights_on(0)
    weights_on(1)
    for copy in rows_there:
        copy.wait_recv()
    weights_done(0)

    def up(n, carry):
        cols = pl.ds(pl.multiple_of(n * tile, tile), tile)
        x = dot(rows[...], win[:, cols], NN)
        c = 0.7978845608028654
        t = jnp.tanh(c * (x + 0.044715 * (x * x * x)))
        side = 0.5 * (1.0 + t)
        hidden[:, cols] = (x * side).astype(BF)
        slope[:, cols] = side + 0.5 * x * (1.0 - t * t) * (c * (1.0 + 3 * 0.044715 * (x * x)))
        return carry

    lax.fori_loop(0, hid // tile, up, 0)

    parts = (part_in, part_out)
    shares = []

    def first_share(a, h, j, i):
        n_one, one, n_two, two = sides_of(h)
        whose = dp_at(i, (two + j) % n_two, h == 0)
        to = dp_at(one, (two + j) % n_two, h == 0)
        return remote(
            parts[a].at[whose, pl.ds(h * half, half)],
            first_got.at[a, h, j - 1, i],
            g_send.at[a, h, j, i],
            g_recv.at[a, h, j, i],
            (to, ex),
        )

    def weight_grad(a, left, right):
        part = parts[a]
        if depth % 128 == 0:
            for i in range(1, n_dp + 1):
                to = (dp + i) % n_dp
                cols = pl.ds(pl.multiple_of(to * depth, depth), depth)
                part[to] = dot(left[:, cols], right[...], TN).astype(BF)
        else:

            def some(n, carry):
                cols = pl.ds(pl.multiple_of(n * tile, tile), tile)
                made = dot(left[:, cols], right[...], TN).astype(BF)
                many = tile // depth
                part[pl.ds(n * many, many)] = made.reshape(many, depth, hid)
                return carry

            lax.fori_loop(0, width // tile, some, 0)
        for h in range(2):
            n_one, _, n_two, _ = sides_of(h)
            for j in range(1, n_two):
                for i in range(n_one):
                    copy = first_share(a, h, j, i)
                    copy.start()
                    shares.append(copy)

    def met(a, h, place):
        n_one, one, n_two, two = sides_of(h)
        value = parts[a][dp_at(place, two, h == 0), pl.ds(h * half, half)].astype(F32)
        for j in range(1, n_two):
            value = value + first_got[a, h, j - 1, place].astype(F32)
        return value

    def second_shares(a):
        for h in range(2):
            n_one, one, n_two, two = sides_of(h)
            for j in range(1, n_two):
                for i in range(n_one):
                    first_share(a, h, j, i).wait_recv()
            for i in range(1, n_one):
                place = (one + i) % n_one
                staged[a, h, i - 1] = met(a, h, place).astype(BF)
                copy = remote(
                    staged.at[a, h, i - 1],
                    second_got.at[a, h, i - 1],
                    h_send.at[a, h, i],
                    h_recv.at[a, h, i],
                    (dp_at(place, two, h == 0), ex),
                )
                copy.start()
                seconds[a].append(copy)

    seconds = ([], [])

    def weight_sum(a, out):
        for copy in seconds[a]:
            copy.wait()
        for h in range(2):
            n_one, one, n_two, two = sides_of(h)
            value = met(a, h, one)
            for i in range(1, n_one):
                value = value + second_got[a, h, i - 1].astype(F32)
            out[pl.ds(h * half, half)] = value

    weights_done(1)

    def down(n, carry):
        cols = pl.ds(pl.multiple_of(n * tile, tile), tile)
        outs[:, cols] = dot(hidden[...], wout[cols, :], NT).astype(BF)
        return carry

    lax.fori_loop(0, width // tile, down, 0)

    outs_back = exchange(2, outs, r_outs)
    for copy in grads_there:
        copy.wait_recv()
    weight_grad(1, grads, hidden)

    def down_grad(n, carry):
        cols = pl.ds(pl.multiple_of(n * tile, tile), tile)
        ghid[:, cols] = (dot(grads[...], wout[:, cols], NN) * slope[:, cols]).astype(BF)
        return carry

    lax.fori_loop(0, hid // tile, down_grad, 0)

    def up_grad(n, carry):
        cols = pl.ds(pl.multiple_of(n * tile, tile), tile)
        back[:, cols] = dot(ghid[...], win[cols, :], NT).astype(BF)
        return carry

    lax.fori_loop(0, width // tile, up_grad, 0)
    grads_back = exchange(3, back, r_back)
    weight_grad(0, rows, ghid)
    second_shares(1)

    for copy in outs_back:
        copy.wait()
    combined = dot(single[0], r_outs[...], TN) * gate_ref[:, 0:1]
    for k in range(1, TOP):
        combined = combined + dot(single[k], r_outs[...], TN) * gate_ref[:, k : k + 1]
    mixed_ref[...] = (patches_ref[...].astype(F32) + combined).astype(BF)
    second_shares(0)

    for copy in grads_back:
        copy.wait()
    unit, scale = normalise(conv[...])
    lean = dot(picked[...], r_back[...], TN) * gain_ref[...]
    inner = lean - jnp.mean(lean, axis=1, keepdims=True)
    inner = inner - unit * jnp.mean(lean * unit, axis=1, keepdims=True)
    fill_pad(pad, inner * scale)
    conv_into(pad, taps_ref, grad_ref, None, True)
    grad_ref[...] += cot_ref[...].astype(F32)

    weight_sum(1, gw_out_ref)
    weight_sum(0, gw_in_ref)
    for copy in started + shares + rows_there + grads_there:
        copy.wait_send()


def grid_of(n_dp):
    side = max(i for i in range(1, n_dp + 1) if n_dp % i == 0 and i * i <= n_dp)
    return side, n_dp // side


def local(
    patches,
    expert_ids,
    gate_weights,
    conv_weight,
    conv_bias,
    ln_gain,
    ln_shift,
    w_in,
    w_out,
    grad_mixed,
):
    tokens, width = patches.shape
    depth, hid = w_in.shape[1:]
    n_exp = lax.axis_size("expert")
    n_dp = lax.axis_size("dp")
    cap = 4 * tokens // n_exp
    count = n_exp * cap
    vmem = pl.BlockSpec(memory_space=pltpu.VMEM)
    dma = pltpu.SemaphoreType.DMA
    long = max(grid_of(n_dp))
    more = max(long - 1, 1)
    half = depth // 2
    mixed, grad_input, gw_in, gw_out = pl.pallas_call(
        functools.partial(moe_body, n_dp, n_exp, cap),
        out_shape=(
            jax.ShapeDtypeStruct((tokens, width), BF),
            jax.ShapeDtypeStruct((tokens, width), F32),
            jax.ShapeDtypeStruct((depth, hid), F32),
            jax.ShapeDtypeStruct((depth, hid), F32),
        ),
        in_specs=[vmem] * 10,
        out_specs=(vmem,) * 4,
        scratch_shapes=[
            pltpu.VMEM((IMG_H + 2 * HALF, IMG_W + 2 * EDGE, width), F32),
            pltpu.VMEM((tokens, width), F32),
            pltpu.VMEM((tokens, width), BF),
            pltpu.VMEM((tokens, 128), F32),
            pltpu.VMEM((count, width), BF),
            pltpu.VMEM((count, width), BF),
            pltpu.VMEM((count, tokens), BF),
            pltpu.VMEM((TOP, count, tokens), BF),
            pltpu.VMEM((width, hid), BF),
            pltpu.VMEM((width, hid), BF),
            pltpu.VMEM((count, width), BF),
            pltpu.VMEM((count, width), BF),
            pltpu.VMEM((count, hid), F32),
            pltpu.VMEM((count, hid), BF),
            pltpu.VMEM((count, hid), BF),
            pltpu.VMEM((count, width), BF),
            pltpu.VMEM((count, width), BF),
            pltpu.VMEM((count, width), BF),
            pltpu.VMEM((count, width), BF),
            pltpu.VMEM((n_dp, depth, hid), BF),
            pltpu.VMEM((n_dp, depth, hid), BF),
            pltpu.VMEM((2, 2, more, long, half, hid), BF),
            pltpu.VMEM((2, 2, more, half, hid), BF),
            pltpu.VMEM((2, 2, more, half, hid), BF),
            dma((2, 2, long, long)),
            dma((2, 2, long, long)),
            dma((4, n_exp)),
            dma((4, n_exp)),
            dma((2, 2, long, long)),
            dma((2, 2, long, long)),
            dma((2, 2, long)),
            dma((2, 2, long)),
        ],
        compiler_params=pltpu.CompilerParams(
            collective_id=0, has_side_effects=True, vmem_limit_bytes=58 << 20
        ),
    )(
        patches,
        expert_ids,
        gate_weights,
        conv_weight,
        conv_bias[None],
        ln_gain[None],
        ln_shift[None],
        w_in[0],
        w_out[0],
        grad_mixed,
    )
    return mixed, grad_input, gw_in[None], gw_out[None]


def solution(mesh):
    rows = P(("dp", "expert"), None)
    split = P("expert", "dp", None)
    return jax.shard_map(
        local,
        mesh=mesh,
        in_specs=(rows, rows, rows, P(), P(), P(), P(), split, split, rows),
        out_specs=(rows, rows, split, split),
        check_vma=False,
    )
```

```python
import functools

import jax
import jax.numpy as jnp
from jax import lax
from jax.experimental import pallas as pl
from jax.experimental.pallas import tpu as pltpu
from jax.sharding import PartitionSpec as P

KSIZE = 7
HALF = KSIZE // 2
TOP = 2
IMG_W = 16
IMG_H = 8
EPS = 1e-06
EDGE = 8
MESH = pl.DeviceIdType.MESH
BF = jnp.bfloat16
F32 = jnp.float32


def conv_into(pad, weight_ref, out_ref, bias_ref, flip):
    width = out_ref.shape[1]

    def chunk(i, carry):
        lanes = pl.ds(pl.multiple_of(i * 128, 128), 128)
        total = jnp.zeros((IMG_H, IMG_W, 128), F32)
        if bias_ref is not None:
            total = total + bias_ref[0:1, lanes].reshape(1, 1, 128)
        for col in range(KSIZE):
            start = EDGE - HALF + col
            slab = pad[:, start : start + IMG_W, lanes]
            for row in range(KSIZE):
                tap = row * KSIZE + col
                if flip:
                    tap = KSIZE * KSIZE - 1 - tap
                total = total + slab[row : row + IMG_H] * weight_ref[tap : tap + 1, lanes].reshape(
                    1, 1, 128
                )
        out_ref[:, lanes] = total.reshape(IMG_H * IMG_W, 128)
        return carry

    lax.fori_loop(0, width // 128, chunk, 0)


def fill_pad(pad, image):
    pad[...] = jnp.zeros_like(pad)
    pad[HALF : HALF + IMG_H, EDGE : EDGE + IMG_W, :] = image.reshape(IMG_H, IMG_W, image.shape[-1])


def normalise(conv):
    centred = conv - jnp.mean(conv, axis=1, keepdims=True)
    spread = jnp.mean(centred * centred, axis=1, keepdims=True)
    scale = lax.rsqrt(spread + EPS)
    return centred * scale, scale


def dot(left, right, dims):
    return lax.dot_general(left, right, (dims, ((), ())), preferred_element_type=F32)


NN = ((1,), (0,))
NT = ((1,), (1,))
TN = ((0,), (0,))


def moe_body(
    n_dp,
    n_exp,
    cap,
    patches_ref,
    ids_ref,
    gate_ref,
    taps_ref,
    bias_ref,
    gain_ref,
    shift_ref,
    w_in_ref,
    w_out_ref,
    cot_ref,
    mixed_ref,
    grad_ref,
    gw_in_ref,
    gw_out_ref,
    pad,
    conv,
    normed,
    meta,
    flip,
    win,
    wout,
    all_n,
    all_c,
    all_m,
    rows,
    grads,
    slope,
    hidden,
    ghid,
    outs,
    back,
    r_outs,
    r_back,
    part_in,
    part_out,
    first_got,
    staged,
    second_got,
    w_send,
    w_recv,
    m_send,
    m_recv,
    line_send,
    line_recv,
    twin_send,
    twin_recv,
    ret_send,
    ret_recv,
    g_send,
    g_recv,
    h_send,
    h_recv,
):
    dp = lax.axis_index("dp")
    ex = lax.axis_index("expert")
    chips = n_exp // 2
    chip = ex // 2
    core = ex % 2
    depth, hid = w_in_ref.shape
    tokens, width = patches_ref.shape
    count = n_exp * cap
    tile = 256
    sides = grid_of(n_dp)
    spot = (dp // sides[1], dp % sides[1])
    half = depth // 2

    def dp_at(first, second, turned):
        return second * sides[1] + first if turned else first * sides[1] + second

    barrier = pltpu.get_barrier_semaphore()
    for i in range(1, n_exp):
        pl.semaphore_signal(
            barrier, inc=1, device_id=(dp, (ex + i) % n_exp), device_id_type=MESH
        )
    for i in range(1, n_dp):
        pl.semaphore_signal(barrier, inc=1, device_id=((dp + i) % n_dp, ex), device_id_type=MESH)
    pl.semaphore_wait(barrier, n_exp - 1 + n_dp - 1)

    def remote(src, dst, send, recv, to):
        return pltpu.make_async_remote_copy(
            src_ref=src, dst_ref=dst, send_sem=send, recv_sem=recv, device_id=to, device_id_type=MESH
        )

    full = (win, wout)
    shard = (w_in_ref, w_out_ref)
    started = []

    def sides_of(h):
        return sides[1 - h], spot[1 - h], sides[h], spot[h]

    def half_at(who, h):
        return pl.ds(pl.multiple_of(who * depth + h * half, 16), half)

    def weight_copy(a, h, i, j, own):
        n_one, one, n_two, two = sides_of(h)
        origin = dp_at((one - i) % n_one, two, h == 0)
        if j == 0:
            to = dp_at((one + i) % n_one, two, h == 0)
            origin = dp
        else:
            to = dp_at(one, (two + j) % n_two, h == 0)
        src = shard[a].at[pl.ds(h * half, half)] if own else full[a].at[half_at(origin, h)]
        return remote(
            src,
            full[a].at[half_at(origin, h)],
            w_send.at[a, h, i, j],
            w_recv.at[a, h, i, j],
            (to, ex),
        )

    def weights_first(a):
        for h in range(2):
            n_one, _, n_two, _ = sides_of(h)
            for i in range(1, n_one):
                copy = weight_copy(a, h, i, 0, True)
                copy.start()
                started.append(copy)
        for h in range(2):
            n_one, _, n_two, _ = sides_of(h)
            for j in range(1, n_two):
                copy = weight_copy(a, h, 0, j, True)
                copy.start()
                started.append(copy)

    def weights_on(a):
        for h in range(2):
            n_one, _, n_two, _ = sides_of(h)
            for i in range(1, n_one):
                weight_copy(a, h, i, 0, True).wait_recv()
                for j in range(1, n_two):
                    copy = weight_copy(a, h, i, j, False)
                    copy.start()
                    started.append(copy)

    def weights_done(a):
        for h in range(2):
            n_one, _, n_two, _ = sides_of(h)
            for i in range(n_one):
                for j in range(1, n_two):
                    weight_copy(a, h, i, j, i == 0).wait_recv()

    own = (normed, cot_ref)
    held = (all_n, all_c)

    def line(a, way, k, src_dev, src):
        step = 1 if way == 0 else -1
        return remote(
            src,
            held[a].at[src_dev],
            line_send.at[a, way, k],
            line_recv.at[a, way, k],
            (dp, jnp.clip(ex + 2 * step, core, n_exp - 2 + core)),
        )

    def twin(a, way, k, src_dev, src):
        return remote(
            src,
            held[a].at[src_dev],
            twin_send.at[a, way, k],
            twin_recv.at[a, way, k],
            (dp, 2 * chip + 1 - core),
        )

    def each(way, k):
        if way == 0:
            return chip - k >= 0, chip + 1 < chips, ex - 2 * k
        return chip + k < chips, chip - 1 >= 0, ex + 2 * k

    def send_step(a, k):
        for way in range(2):
            there, ahead, src_dev = each(way, k)
            src_dev = jnp.clip(src_dev, 0, n_exp - 1)
            src = own[a] if k == 0 else held[a].at[src_dev]
            if k > 0:

                @pl.when(there)
                def _(a=a, way=way, k=k, src_dev=src_dev, src=src):
                    line(a, way, k - 1, src_dev, src).wait_recv()

            if k < chips - 1:

                @pl.when(jnp.logical_and(there, ahead))
                def _(a=a, way=way, k=k, src_dev=src_dev, src=src):
                    line(a, way, k, src_dev, src).start()

            if k > 0:

                @pl.when(there)
                def _(a=a, way=way, k=k, src_dev=src_dev, src=src):
                    twin(a, way, k, src_dev, src).start()

            elif way == 1:
                twin(a, 0, k, src_dev, src).start()

    def finish_twins(a):
        for k in range(chips):
            for way in range(2):
                if k == 0 and way == 1:
                    continue
                there, _, src_dev = each(way, k)
                other = jnp.clip(src_dev + 1 - 2 * core, 0, n_exp - 1)

                @pl.when(there)
                def _(a=a, way=way, k=k, other=other):
                    twin(a, way, k, other, held[a].at[other]).wait_recv()

    def finish_sends(a):
        for k in range(chips):
            for way in range(2):
                there, ahead, src_dev = each(way, k)
                src_dev = jnp.clip(src_dev, 0, n_exp - 1)
                if k < chips - 1:

                    @pl.when(jnp.logical_and(there, ahead))
                    def _(a=a, way=way, k=k, src_dev=src_dev):
                        line(a, way, k, src_dev, own[a]).wait_send()

                if k > 0 or way == 0:

                    @pl.when(there)
                    def _(a=a, way=way, k=k, src_dev=src_dev):
                        twin(a, way, k, src_dev, own[a]).wait_send()

    send_step(1, 0)
    weights_first(0)
    weights_first(1)

    fill_pad(pad, patches_ref[...].astype(F32))
    conv_into(pad, taps_ref, conv, bias_ref, False)
    unit, _ = normalise(conv[...])
    normed[...] = (unit * gain_ref[...] + shift_ref[...]).astype(BF)
    send_step(0, 0)
    if chips > 1:
        send_step(1, 1)

    flip[...] = jnp.zeros_like(flip)
    flip[:, 0:TOP] = ids_ref[...].astype(F32)
    flip[:, TOP : 2 * TOP] = gate_ref[...]
    turned = jnp.transpose(flip[...])
    names = lax.broadcasted_iota(jnp.int32, (n_exp, tokens), 0).astype(F32)
    named = [jnp.where(names == turned[k : k + 1, :], 1.0, 0.0) for k in range(TOP)]
    before = lax.broadcasted_iota(jnp.int32, (tokens, tokens), 0) < lax.broadcasted_iota(
        jnp.int32, (tokens, tokens), 1
    )
    table = named[0]
    for k in range(1, TOP):
        table = table + named[k]
    rank = dot(table.astype(BF), jnp.where(before, 1.0, 0.0).astype(BF), NN)
    places = [
        turned[k : k + 1, :] * cap + jnp.sum(named[k] * rank, axis=0, keepdims=True)
        for k in range(TOP)
    ]
    meta[...] = jnp.zeros_like(meta)
    for k in range(TOP):
        meta[k : k + 1, :] = places[k]
        meta[TOP + k : TOP + k + 1, :] = turned[TOP + k : TOP + k + 1, :]
    metas = []
    for i in range(1, n_exp):
        copy = remote(meta, all_m.at[ex], m_send.at[i], m_recv.at[i], (dp, (ex + i) % n_exp))
        copy.start()
        metas.append(copy)

    mine = pl.ds(pl.multiple_of(dp * depth, 16), depth)
    win[mine] = w_in_ref[...]
    wout[mine] = w_out_ref[...]
    all_n[ex] = normed[...]
    all_c[ex] = cot_ref[...]
    all_m[ex] = meta[...]
    for k in range(1, max(chips, 2)):
        if 1 < k < chips:
            send_step(1, k)
        if k == 1:
            weights_on(0)
        if k < chips:
            send_step(0, k)
        if k == 1:
            weights_on(1)
    for copy in metas:
        copy.wait()

    slots = lax.broadcasted_iota(jnp.int32, (cap, tokens), 0).astype(F32) + (ex * cap).astype(F32)

    def choose(j):
        info = all_m[j]
        hits = [jnp.where(slots == info[k : k + 1, :], 1.0, 0.0) for k in range(TOP)]
        weighed = hits[0] * info[TOP : TOP + 1, :]
        for k in range(1, TOP):
            weighed = weighed + hits[k] * info[TOP + k : TOP + k + 1, :]
        select = hits[0]
        for k in range(1, TOP):
            select = select + hits[k]
        return select.astype(BF), jnp.sum(weighed, axis=1, keepdims=True)

    finish_twins(1)

    def gather_grads(j, carry):
        select, gate = choose(j)
        at = pl.ds(pl.multiple_of(j * cap, 16), cap)
        grads[at] = (dot(select, all_c[j], NN) * gate).astype(BF)
        return carry

    lax.fori_loop(0, n_exp, gather_grads, 0)
    finish_twins(0)

    def gather_rows(j, carry):
        select, _ = choose(j)
        at = pl.ds(pl.multiple_of(j * cap, 16), cap)
        rows[at] = dot(select, all_n[j], NN).astype(BF)
        return carry

    lax.fori_loop(0, n_exp, gather_rows, 0)
    weights_done(0)

    def up(n, carry):
        cols = pl.ds(pl.multiple_of(n * tile, tile), tile)
        x = dot(rows[...], win[:, cols], NN)
        c = 0.7978845608028654
        t = jnp.tanh(c * (x + 0.044715 * (x * x * x)))
        side = 0.5 * (1.0 + t)
        hidden[:, cols] = (x * side).astype(BF)
        slope[:, cols] = side + 0.5 * x * (1.0 - t * t) * (c * (1.0 + 3 * 0.044715 * (x * x)))
        return carry

    lax.fori_loop(0, hid // tile, up, 0)

    parts = (part_in, part_out)
    shares = []

    def first_share(a, h, j, i):
        n_one, one, n_two, two = sides_of(h)
        whose = dp_at(i, (two + j) % n_two, h == 0)
        to = dp_at(one, (two + j) % n_two, h == 0)
        return remote(
            parts[a].at[whose, pl.ds(h * half, half)],
            first_got.at[a, h, j - 1, i],
            g_send.at[a, h, j, i],
            g_recv.at[a, h, j, i],
            (to, ex),
        )

    def weight_grad(a, left, right):
        part = parts[a]
        if depth % 128 == 0:
            for i in range(1, n_dp + 1):
                to = (dp + i) % n_dp
                cols = pl.ds(pl.multiple_of(to * depth, depth), depth)
                part[to] = dot(left[:, cols], right[...], TN).astype(BF)
        else:

            def some(n, carry):
                cols = pl.ds(pl.multiple_of(n * tile, tile), tile)
                made = dot(left[:, cols], right[...], TN).astype(BF)
                many = tile // depth
                part[pl.ds(n * many, many)] = made.reshape(many, depth, hid)
                return carry

            lax.fori_loop(0, width // tile, some, 0)
        for h in range(2):
            n_one, _, n_two, _ = sides_of(h)
            for j in range(1, n_two):
                for i in range(n_one):
                    copy = first_share(a, h, j, i)
                    copy.start()
                    shares.append(copy)

    def met(a, h, place):
        n_one, one, n_two, two = sides_of(h)
        value = parts[a][dp_at(place, two, h == 0), pl.ds(h * half, half)].astype(F32)
        for j in range(1, n_two):
            value = value + first_got[a, h, j - 1, place].astype(F32)
        return value

    def second_shares(a):
        for h in range(2):
            n_one, one, n_two, two = sides_of(h)
            for j in range(1, n_two):
                for i in range(n_one):
                    first_share(a, h, j, i).wait_recv()
            for i in range(1, n_one):
                place = (one + i) % n_one
                staged[a, h, i - 1] = met(a, h, place).astype(BF)
                copy = remote(
                    staged.at[a, h, i - 1],
                    second_got.at[a, h, i - 1],
                    h_send.at[a, h, i],
                    h_recv.at[a, h, i],
                    (dp_at(place, two, h == 0), ex),
                )
                copy.start()
                seconds[a].append(copy)

    seconds = ([], [])

    def weight_sum(a, out):
        for copy in seconds[a]:
            copy.wait()
        for h in range(2):
            n_one, one, n_two, two = sides_of(h)
            value = met(a, h, one)
            for i in range(1, n_one):
                value = value + second_got[a, h, i - 1].astype(F32)
            out[pl.ds(h * half, half)] = value

    weights_done(1)

    def down(n, carry):
        cols = pl.ds(pl.multiple_of(n * tile, tile), tile)
        outs[:, cols] = dot(hidden[...], wout[cols, :], NT).astype(BF)
        return carry

    lax.fori_loop(0, width // tile, down, 0)

    my_rows = pl.ds(pl.multiple_of(ex * cap, 16), cap)

    def give_back(a, src, dst):
        copies = []
        for i in range(1, n_exp):
            to = (ex + i) % n_exp
            copy = remote(
                src.at[pl.ds(pl.multiple_of(to * cap, 16), cap)],
                dst.at[my_rows],
                ret_send.at[a, i],
                ret_recv.at[a, i],
                (dp, to),
            )
            copy.start()
            copies.append(copy)
        dst[my_rows] = src[my_rows]
        return copies

    outs_back = give_back(0, outs, r_outs)
    weight_grad(1, grads, hidden)

    def down_grad(n, carry):
        cols = pl.ds(pl.multiple_of(n * tile, tile), tile)
        ghid[:, cols] = (dot(grads[...], wout[:, cols], NN) * slope[:, cols]).astype(BF)
        return carry

    lax.fori_loop(0, hid // tile, down_grad, 0)

    def up_grad(n, carry):
        cols = pl.ds(pl.multiple_of(n * tile, tile), tile)
        back[:, cols] = dot(ghid[...], win[cols, :], NT).astype(BF)
        return carry

    lax.fori_loop(0, width // tile, up_grad, 0)
    grads_back = give_back(1, back, r_back)
    weight_grad(0, rows, ghid)
    second_shares(1)

    tall = lax.broadcasted_iota(jnp.int32, (count, tokens), 0).astype(F32)
    ones = [jnp.where(tall == meta[k : k + 1, :], 1.0, 0.0).astype(BF) for k in range(TOP)]
    for copy in outs_back:
        copy.wait()
    combined = dot(ones[0], r_outs[...], TN) * gate_ref[:, 0:1]
    for k in range(1, TOP):
        combined = combined + dot(ones[k], r_outs[...], TN) * gate_ref[:, k : k + 1]
    mixed_ref[...] = (patches_ref[...].astype(F32) + combined).astype(BF)
    second_shares(0)

    for copy in grads_back:
        copy.wait()
    both = ones[0]
    for k in range(1, TOP):
        both = both + ones[k]
    unit, scale = normalise(conv[...])
    lean = dot(both, r_back[...], TN) * gain_ref[...]
    inner = lean - jnp.mean(lean, axis=1, keepdims=True)
    inner = inner - unit * jnp.mean(lean * unit, axis=1, keepdims=True)
    fill_pad(pad, inner * scale)
    conv_into(pad, taps_ref, grad_ref, None, True)
    grad_ref[...] += cot_ref[...].astype(F32)

    weight_sum(1, gw_out_ref)
    weight_sum(0, gw_in_ref)
    for copy in started + shares:
        copy.wait_send()
    finish_sends(0)
    finish_sends(1)


def grid_of(n_dp):
    side = max(i for i in range(1, n_dp + 1) if n_dp % i == 0 and i * i <= n_dp)
    return side, n_dp // side


def local(
    patches,
    expert_ids,
    gate_weights,
    conv_weight,
    conv_bias,
    ln_gain,
    ln_shift,
    w_in,
    w_out,
    grad_mixed,
):
    tokens, width = patches.shape
    depth, hid = w_in.shape[1:]
    n_exp = lax.axis_size("expert")
    n_dp = lax.axis_size("dp")
    cap = 4 * tokens // n_exp
    count = n_exp * cap
    vmem = pl.BlockSpec(memory_space=pltpu.VMEM)
    dma = pltpu.SemaphoreType.DMA
    chips = n_exp // 2
    long = max(grid_of(n_dp))
    more = max(long - 1, 1)
    half = depth // 2
    mixed, grad_input, gw_in, gw_out = pl.pallas_call(
        functools.partial(moe_body, n_dp, n_exp, cap),
        out_shape=(
            jax.ShapeDtypeStruct((tokens, width), BF),
            jax.ShapeDtypeStruct((tokens, width), F32),
            jax.ShapeDtypeStruct((depth, hid), F32),
            jax.ShapeDtypeStruct((depth, hid), F32),
        ),
        in_specs=[vmem] * 10,
        out_specs=(vmem,) * 4,
        scratch_shapes=[
            pltpu.VMEM((IMG_H + 2 * HALF, IMG_W + 2 * EDGE, width), F32),
            pltpu.VMEM((tokens, width), F32),
            pltpu.VMEM((tokens, width), BF),
            pltpu.VMEM((8, tokens), F32),
            pltpu.VMEM((tokens, 128), F32),
            pltpu.VMEM((width, hid), BF),
            pltpu.VMEM((width, hid), BF),
            pltpu.VMEM((n_exp, tokens, width), BF),
            pltpu.VMEM((n_exp, tokens, width), BF),
            pltpu.VMEM((n_exp, 8, tokens), F32),
            pltpu.VMEM((count, width), BF),
            pltpu.VMEM((count, width), BF),
            pltpu.VMEM((count, hid), F32),
            pltpu.VMEM((count, hid), BF),
            pltpu.VMEM((count, hid), BF),
            pltpu.VMEM((count, width), BF),
            pltpu.VMEM((count, width), BF),
            pltpu.VMEM((count, width), BF),
            pltpu.VMEM((count, width), BF),
            pltpu.VMEM((n_dp, depth, hid), BF),
            pltpu.VMEM((n_dp, depth, hid), BF),
            pltpu.VMEM((2, 2, more, long, half, hid), BF),
            pltpu.VMEM((2, 2, more, half, hid), BF),
            pltpu.VMEM((2, 2, more, half, hid), BF),
            dma((2, 2, long, long)),
            dma((2, 2, long, long)),
            dma((n_exp,)),
            dma((n_exp,)),
            dma((2, 2, chips)),
            dma((2, 2, chips)),
            dma((2, 2, chips)),
            dma((2, 2, chips)),
            dma((2, n_exp)),
            dma((2, n_exp)),
            dma((2, 2, long, long)),
            dma((2, 2, long, long)),
            dma((2, 2, long)),
            dma((2, 2, long)),
        ],
        compiler_params=pltpu.CompilerParams(
            collective_id=0, has_side_effects=True, vmem_limit_bytes=58 << 20
        ),
    )(
        patches,
        expert_ids,
        gate_weights,
        conv_weight,
        conv_bias[None],
        ln_gain[None],
        ln_shift[None],
        w_in[0],
        w_out[0],
        grad_mixed,
    )
    return mixed, grad_input, gw_in[None], gw_out[None]


def solution(mesh):
    rows = P(("dp", "expert"), None)
    split = P("expert", "dp", None)
    return jax.shard_map(
        local,
        mesh=mesh,
        in_specs=(rows, rows, rows, P(), P(), P(), P(), split, split, rows),
        out_specs=(rows, rows, split, split),
        check_vma=False,
    )
```
